32 devices in a mesh: section: 4 (over z), req: 4 (over y, x), tp: 2 (over core).
Axes of the slice: x: 2, y: 2, z: 4, core: 2. Of those that a mesh axis runs over, the one named last changes fastest.
Arguments:
- hidden: bfloat16 [4, 4, 64, 8192], P(None, 'section', 'req', 'tp'), may hold values from -6 to 6
- norm_gain: bfloat16 [4, 8192], P('section', 'tp'), may hold values from 0.099609375 to 1.8984375
- w_kv: bfloat16 [4, 8192, 2, 1024], P('section', None, None, 'tp'), may hold values from -0.0625 to 0.0625
- queries: bfloat16 [4, 4, 64, 8192], P(None, 'section', 'req', 'tp'), may hold values from -120 to 120
- cache_kv: bfloat16 [4, 64, 2, 128, 1024], P('section', 'req', None, None, 'tp'), may hold values from -4 to 4
- exits: int32 [4, 64], P(None, 'req'), may hold values from 0 to 4, as said below
- lengths: int32 [64], P('req'), may hold values from 2 to 124, as said below
Outputs:
- attn_out: bfloat16 [4, 4, 64, 8192], P(None, 'section', 'req', 'tp')
- new_kv: bfloat16 [4, 4, 64, 2, 1024], P(None, 'section', 'req', None, 'tp')
The draws below stay inside these ranges and needn't reach their ends.
Inputs may be any that keep to these rules, and one draw needn't show every extreme that they name: `exits`: in each step, among the 16 requests of each aligned block, no layer below 4 is named by more than 2 requests, some layer below 4 is named by exactly 2, and some request names 4. `lengths`: every aligned block of 16 requests holds a request of length 124.
All inputs are finite; a program needn't handle non-finite values.
Results may differ from the reference program's by a relative error of at most 0.0056.
Values may be sent and summed in bfloat16 or wider, within the bound.
A program may use at most 128 MiB of HBM per device.

```python
import jax
import jax.numpy as jnp
from jax import lax

D = 8192
Q_HEADS = 64
KV_HEADS = 8
HEAD = 128
REQ_DEV = 16
CACHE = 128
STEPS = 4
EXIT_CAP = 2
LAYERS = 4
REQUESTS = 64


def shared_first_keys(key):
    return jnp.clip(jax.random.normal(jax.random.fold_in(key, 7), (LAYERS, REQUESTS, KV_HEADS, HEAD), jnp.float32), -4.0, 4.0)


def draw_cache_kv(key, part):
    first_keys = shared_first_keys(key)
    entries = jnp.clip(jax.random.normal(jax.random.fold_in(key, 11), (LAYERS, REQUESTS, 2, CACHE, KV_HEADS, HEAD), jnp.float32), -4.0, 4.0)
    entries = entries.at[:, :, 0, 0].set(first_keys)
    return entries.reshape(LAYERS, REQUESTS, 2, CACHE, KV_HEADS * HEAD).astype(jnp.bfloat16)


def draw_queries(key, part):
    groups = Q_HEADS // KV_HEADS
    entries = jnp.clip(jax.random.normal(jax.random.fold_in(key, 13), (STEPS, LAYERS, REQUESTS, KV_HEADS, groups, HEAD), jnp.float32), -4.0, 4.0)
    return entries.reshape(STEPS, LAYERS, REQUESTS, Q_HEADS * HEAD).astype(jnp.bfloat16)


def exit_block(block_key, block_number):
    drawn_layer = jax.random.randint(jax.random.fold_in(block_key, 1), (), 0, LAYERS).astype(jnp.int32)
    chosen = jnp.where(block_number == 0, 0, drawn_layer).astype(jnp.int32)
    base_pool = jnp.repeat(jnp.arange(0, LAYERS, dtype=jnp.int32), EXIT_CAP)
    base_pool = jnp.where(base_pool == chosen, LAYERS, base_pool).astype(jnp.int32)
    full_pool = jnp.concatenate([base_pool, jnp.full((REQ_DEV // 2,), LAYERS, jnp.int32)])
    full_pool = jax.random.permutation(jax.random.fold_in(block_key, 2), full_pool)
    picked = jnp.concatenate([full_pool[:REQ_DEV - EXIT_CAP - 1], jnp.zeros((EXIT_CAP,), jnp.int32) + chosen, jnp.full((1,), LAYERS, jnp.int32)])
    return jax.random.permutation(jax.random.fold_in(block_key, 3), picked)


def draw_exits(key, part):
    shards = REQUESTS // REQ_DEV
    block_keys = jax.random.split(jax.random.fold_in(key, 21), STEPS * shards)
    block_numbers = jnp.arange(STEPS * shards, dtype=jnp.int32)
    return jax.vmap(exit_block)(block_keys, block_numbers).reshape(STEPS, REQUESTS).astype(jnp.int32)


def draw_lengths(key, part):
    shards = REQUESTS // REQ_DEV
    drawn = jax.random.randint(jax.random.fold_in(key, 31), (shards, REQ_DEV), 2, CACHE - STEPS + 1)
    longest = jax.random.randint(jax.random.fold_in(key, 32), (shards, 1), 0, REQ_DEV)
    drawn = jnp.where(jnp.arange(REQ_DEV)[None, :] == longest, CACHE - STEPS, drawn)
    return drawn.reshape(REQUESTS).astype(jnp.int32)


def shard_levels(rng, dims, pieces, least, high):
    factor_of, own = 1.0, jax.random.fold_in(rng, 6)
    for axis_at, shards_of in pieces:
        draws = jnp.exp(jax.random.uniform(jax.random.fold_in(own, axis_at), (shards_of,), jnp.float32, least / len(pieces), high / len(pieces)))
        factor_of = factor_of * jnp.repeat(draws, dims[axis_at] // shards_of).reshape([-1 if axis == axis_at else 1 for axis in range(len(dims))])
    return factor_of


def bell_draw(rng, dims, scale, reach, cuts=(), held_as=jnp.bfloat16):
    array = scale * jax.random.normal(rng, dims, jnp.float32)
    if cuts:
        array = array * shard_levels(rng, dims, cuts, -0.22, 0.18)
    return jnp.clip(array, -reach, reach).astype(held_as)


def setup_inputs(seed: int = 0) -> dict:
    key_of = jax.random.split(jax.random.key(seed), 8)
    hidden = bell_draw(key_of[0], (STEPS, LAYERS, REQUESTS, D), 1.0, 6.0, ((1, 4), (2, 4), (3, 2)))
    norm_gain = jnp.clip(1.0 + 0.18 * jax.random.normal(key_of[1], (LAYERS, D), jnp.float32), 0.099609375, 1.8984375).astype(jnp.bfloat16)
    w_kv = bell_draw(key_of[2], (LAYERS, D, 2, KV_HEADS * HEAD), D ** -0.5, 0.0625, ((0, 4), (3, 2)))
    queries = draw_queries(jax.random.fold_in(key_of[7], 71), 0)
    cache_kv = draw_cache_kv(jax.random.fold_in(key_of[7], 71), 0)
    exits = draw_exits(jax.random.fold_in(key_of[7], 71), 0)
    lengths = draw_lengths(jax.random.fold_in(key_of[7], 71), 0)
    return dict(hidden=hidden, norm_gain=norm_gain, w_kv=w_kv, queries=queries, cache_kv=cache_kv, exits=exits, lengths=lengths)


EPSILON = 1e-05
ROPE_BASE = 500000.0

def apply_rotary(key_heads, positions):
    half_width = key_heads.shape[-1] // 2
    exponent = jnp.arange(half_width, dtype=jnp.float32) * (2.0 / key_heads.shape[-1])
    frequency = ROPE_BASE ** (-exponent)
    angles = positions.astype(jnp.float32)[..., None, None] * frequency
    cosine = jnp.cos(angles)
    sine_part = jnp.sin(angles)
    lower = key_heads[..., :half_width]
    upper = key_heads[..., half_width:]
    return jnp.concatenate([lower * cosine - upper * sine_part, upper * cosine + lower * sine_part], axis=-1)

def reference(hidden, norm_gain, w_kv, queries, cache_kv, exits, lengths):
    num_steps = hidden.shape[0]
    num_layers = hidden.shape[1]
    num_reqs = hidden.shape[2]
    width = hidden.shape[3]
    kv_width = w_kv.shape[-1]
    kv_heads = kv_width // HEAD
    groups = queries.shape[-1] // kv_width
    cache_len = cache_kv.shape[3]
    positions = lengths[None, :] + jnp.arange(num_steps, dtype=jnp.int32)[:, None]
    slot_ids = jnp.arange(cache_len, dtype=jnp.int32)
    step_ids = jnp.arange(num_steps, dtype=jnp.int32)[:, None]
    req_ids = jnp.arange(num_reqs, dtype=jnp.int32)[None, :]
    outputs = []
    written_kv = []
    for layer in range(num_layers):
        source = hidden[step_ids, jnp.minimum(exits, layer).astype(jnp.int32), req_ids]
        values_in = source.astype(jnp.float32)
        inverse = lax.rsqrt(lax.optimization_barrier(jnp.mean(values_in * values_in, axis=-1, keepdims=True)) + EPSILON)
        normed = (values_in * inverse * norm_gain[layer].astype(jnp.float32)).astype(jnp.bfloat16)
        pairs = jnp.dot(normed.reshape(num_steps * num_reqs, width), w_kv[layer].reshape(width, 2 * kv_width), preferred_element_type=jnp.float32)
        pairs = pairs.reshape(num_steps, num_reqs, 2, kv_heads, HEAD)
        new_keys = apply_rotary(pairs[:, :, 0], positions).astype(jnp.bfloat16)
        new_values = pairs[:, :, 1].astype(jnp.bfloat16)
        fresh_kv = jnp.stack([new_keys, new_values], axis=2).reshape(num_steps, num_reqs, 2, kv_width)
        written_kv.append(fresh_kv)
        kv_cache = cache_kv[layer]
        for step_index in range(num_steps):
            written = slot_ids[None, :] == positions[step_index][:, None]
            kv_cache = jnp.where(written[:, None, :, None], fresh_kv[step_index][:, :, None, :], kv_cache)
        all_keys = kv_cache[:, 0].reshape(num_reqs, cache_len, kv_heads, HEAD).astype(jnp.float32)
        all_values = kv_cache[:, 1].reshape(num_reqs, cache_len, kv_heads, HEAD).astype(jnp.float32)
        query_heads = queries[:, layer].reshape(num_steps, num_reqs, kv_heads, groups, HEAD).astype(jnp.float32)
        scores = jnp.einsum('trkgd,rckd->trkgc', query_heads, all_keys) * HEAD ** (-0.5)
        visible = slot_ids[None, None, :] <= positions[:, :, None]
        scores = jnp.where(visible[:, :, None, None, :], scores, -1e+30)
        top_score = lax.optimization_barrier(jnp.max(scores, axis=-1, keepdims=True))
        weights = jnp.exp(scores - top_score)
        weights = (weights / lax.optimization_barrier(jnp.sum(weights, axis=-1, keepdims=True))).astype(jnp.bfloat16)
        weights = lax.optimization_barrier(weights).astype(jnp.float32)
        attended = jnp.einsum('trkgc,rckd->trkgd', weights, all_values)
        live_mask = (layer < exits).astype(jnp.float32)
        attended = attended * live_mask[:, :, None, None, None]
        outputs.append(attended.reshape(num_steps, num_reqs, groups * kv_width).astype(jnp.bfloat16))
    return (jnp.stack(outputs, axis=1), jnp.stack(written_kv, axis=1))
```

```python
import functools
import math

import jax
import jax.numpy as jnp
from jax import lax
from jax.experimental import pallas as pl
from jax.experimental.pallas import tpu as pltpu
from jax.sharding import PartitionSpec as P

HEAD = 128
EXIT_CAP = 2
EPSILON = 1e-05
ROPE_BASE = 500000.0
CHUNKS = 4
BF = jnp.bfloat16
F32 = jnp.float32
MESH = pl.DeviceIdType.MESH


def iota(shape, axis):
    return lax.broadcasted_iota(jnp.int32, shape, axis)


def kernel(S, TP, hid, gain, w_hbm, q_hbm, c_hbm, ecol, erow, pos, lens,
           out, kvout,
           wv, cv, qv, qs, os, ms, ls, xf, gb, pack, gsend, gfull, lk, acc,
           wsem, csem, qsem, sec_send, sec_recv, x_send, x_recv, g_send, g_recv, f_send, f_recv):
    T, R, Dl = hid.shape
    D, _, N = w_hbm.shape
    nt = N // HEAD
    M = T * R
    half = Dl // 2
    rows = T * EXIT_CAP
    slot = 2 * rows
    C = c_hbm.shape[2]
    HG = qs.shape[2]
    G = HG // nt
    sec = lax.axis_index("section")
    req = lax.axis_index("req")
    tp = lax.axis_index("tp")

    barrier = pltpu.get_barrier_semaphore()
    for d in range(1, S):
        pl.semaphore_signal(barrier, inc=1, device_id=(lax.rem(sec + d, S), req, tp), device_id_type=MESH)
    for d in range(1, TP):
        pl.semaphore_signal(barrier, inc=1, device_id=(sec, req, lax.rem(tp + d, TP)), device_id_type=MESH)

    q_copy = pltpu.make_async_copy(q_hbm, qv, qsem)
    q_copy.start()
    c_copies = [pltpu.make_async_copy(c_hbm.at[pl.ds(i * (R // 2), R // 2)], cv.at[pl.ds(i * (R // 2), R // 2)], csem.at[i])
                for i in range(2)]
    for c in c_copies:
        c.start()
    cd = D // CHUNKS

    def w_copy(c, n):
        return pltpu.make_async_copy(
            w_hbm.at[pl.ds(c * cd, cd), :, pl.ds(n * HEAD, HEAD)],
            wv.at[n, pl.ds(c * cd, cd)], wsem.at[c, n])

    for c in range(CHUNKS):
        for n in range(nt):
            w_copy(c, n).start()

    ec = ecol[...]
    er = erow[...]
    ri, rj = iota((M, M), 0), iota((M, M), 1)
    same = (ec == er) & (ri // R == rj // R)
    rank_row = jnp.sum((same & (ri < rj)).astype(F32), axis=0, keepdims=True).astype(jnp.int32)
    rank_col = jnp.sum((same & (rj < ri)).astype(F32), axis=1, keepdims=True).astype(jnp.int32)
    pk, pj = iota((rows, M), 0), iota((rows, M), 1)
    pick = ((er == sec) & (pk == (pj // R) * EXIT_CAP + rank_row)).astype(F32).astype(BF)
    hv = hid[...].reshape(M, Dl)
    packed = jnp.dot(pick, hv, preferred_element_type=F32)
    pack[...] = jnp.concatenate([packed[:, :half], packed[:, half:]], axis=0).astype(BF)
    gsend[...] = jnp.broadcast_to(gain[...].astype(F32), gsend.shape)
    pl.semaphore_wait(barrier, S - 1 + TP - 1)

    def sec_copy(d, src, target):
        return pltpu.make_async_remote_copy(
            src_ref=pack, dst_ref=gb.at[tp, pl.ds(src * slot, slot)],
            send_sem=sec_send.at[d - 1], recv_sem=sec_recv.at[d - 1],
            device_id=(target, req, tp), device_id_type=MESH)

    for d in range(1, S):
        @pl.when(sec + d < S)
        def _():
            sec_copy(d, sec, lax.rem(sec + d, S)).start()

    def x_copy(d):
        return pltpu.make_async_remote_copy(
            src_ref=hid, dst_ref=xf.at[tp], send_sem=x_send.at[d - 1], recv_sem=x_recv.at[d - 1],
            device_id=(sec, req, lax.rem(tp + d, TP)), device_id_type=MESH)

    def g_copy(d):
        return pltpu.make_async_remote_copy(
            src_ref=gsend, dst_ref=gfull.at[tp], send_sem=g_send.at[d - 1], recv_sem=g_recv.at[d - 1],
            device_id=(sec, req, lax.rem(tp + d, TP)), device_id_type=MESH)

    for d in range(1, TP):
        x_copy(d).start()
        g_copy(d).start()
    xf[tp] = hid[...]
    gfull[tp] = gsend[...]
    for s in range(S):
        @pl.when(s >= sec)
        def _():
            gb[:, s * slot:(s + 1) * slot, :] = jnp.zeros((TP, slot, half), BF)

    def fwd_copy(s, o, d):
        span = pl.ds(s * slot, slot)
        return pltpu.make_async_remote_copy(
            src_ref=gb.at[tp, span], dst_ref=gb.at[tp, span],
            send_sem=f_send.at[o - 1, d - 1], recv_sem=f_recv.at[o - 1, d - 1],
            device_id=(sec, req, lax.rem(tp + d, TP)), device_id_type=MESH)

    q_copy.wait()
    for t in range(T):
        for j in range(HG):
            qs[t, :, j, :] = qv[t, :, j * HEAD:(j + 1) * HEAD].astype(F32)

    for d in range(1, S):
        @pl.when(sec - d >= 0)
        def _():
            s = lax.rem(sec - d + S, S)
            sec_copy(d, s, lax.rem(sec + d, S)).wait_recv()
            for e in range(1, TP):
                fwd_copy(s, d, e).start()

    for c in c_copies:
        c.wait()
    scale = HEAD ** -0.5
    RB = 2

    def old(i, _):
        for b in range(RB):
            r = i * RB + b
            seen = iota((T * G, C), 1) < lens[r]
            for h in range(nt):
                hs = slice(h * G, (h + 1) * G)
                cs = slice(h * HEAD, (h + 1) * HEAD)
                qh = jnp.concatenate([qs[t, r, hs, :] for t in range(T)], axis=0).astype(BF)
                s = lax.dot_general(qh, cv[r, 0, :, cs], (((1,), (1,)), ((), ())), preferred_element_type=F32) * scale
                s = jnp.where(seen, s, -1e30)
                m = jnp.max(s, axis=1, keepdims=True)
                p = jnp.exp(s - m)
                l = jnp.broadcast_to(jnp.sum(p, axis=1, keepdims=True), (T * G, HEAD))
                m = jnp.broadcast_to(m, (T * G, HEAD))
                o = jnp.dot(p.astype(BF), cv[r, 1, :, cs], preferred_element_type=F32)
                for t in range(T):
                    g = slice(t * G, (t + 1) * G)
                    os[t, r, hs, :] = o[g]
                    ms[t, r, hs, :] = m[g]
                    ls[t, r, hs, :] = l[g]
        return 0

    lax.fori_loop(0, R // RB, old, 0)

    lane = iota((M, HEAD), 1)
    exponent = lax.rem(lane, HEAD // 2).astype(F32) * (2.0 / HEAD)
    angle = pos[...].astype(F32) * jnp.exp(exponent * (-math.log(ROPE_BASE)))
    cosine = jnp.cos(angle)
    sine = jnp.where(lane < HEAD // 2, -1.0, 1.0) * jnp.sin(angle)

    for d in range(1, TP):
        x_copy(d).wait_recv()
        g_copy(d).wait_recv()
    for d in range(1, S):
        @pl.when(sec - d >= 0)
        def _():
            for e in range(1, TP):
                fwd_copy(lax.rem(sec - d + S, S), d, e).wait_recv()

    want = ec * slot + (iota((M, 1), 0) // R) * EXIT_CAP + rank_col
    skipped = ec < sec
    W = min(half, 512)
    total = jnp.zeros((M, HEAD), F32)
    for f in range(2):
        choose = (iota((M, S * slot), 1) == want + f * rows).astype(F32).astype(BF)
        for p in range(TP):
            def part(i, total, f=f, p=p, choose=choose):
                gc = pl.ds(pl.multiple_of(i * W, W), W)
                xc = pl.ds(pl.multiple_of(f * half + i * W, W), W)
                came = jnp.dot(choose, gb[p, :, gc], preferred_element_type=F32)
                src = jnp.where(skipped, came, xf[p, :, :, xc].reshape(M, W).astype(F32))
                xf[p, :, :, xc] = src.astype(BF).reshape(T, R, W)
                for k in range(W // HEAD):
                    v = src[:, k * HEAD:(k + 1) * HEAD]
                    total = total + v * v
                return total
            total = lax.fori_loop(0, half // W, part, total)
    inverse = lax.rsqrt(jnp.sum(total, axis=1, keepdims=True) / D + EPSILON)

    er_, ec_ = iota((HEAD, 2 * HEAD), 0), iota((HEAD, 2 * HEAD), 1)
    even = (ec_ == 2 * er_).astype(F32).astype(BF)
    odd = (ec_ == 2 * er_ + 1).astype(F32).astype(BF)
    B = 8
    for p in range(TP):
        def expand(i, _, p=p):
            parts = []
            for b in range(B):
                cols = pl.ds(pl.multiple_of((i * B + b) * HEAD, HEAD), HEAD)
                v = xf[p, :, :, cols].reshape(M, HEAD).astype(F32) * inverse * gfull[p, 0:1, cols]
                parts.append(v.astype(BF))
            x = jnp.concatenate(parts, axis=0)
            a = jnp.dot(x, even, preferred_element_type=F32).astype(BF)
            c = jnp.dot(x, odd, preferred_element_type=F32).astype(BF)
            for b in range(B):
                cols = pl.ds(pl.multiple_of((p * (Dl // HEAD) + i * B + b) * 2 * HEAD, 2 * HEAD), 2 * HEAD)
                lk[0:M, cols] = a[b * M:(b + 1) * M]
                lk[M:2 * M, cols] = c[b * M:(b + 1) * M]
            return 0
        lax.fori_loop(0, Dl // HEAD // B, expand, 0)

    wf = wv.reshape(nt, 2 * D, HEAD)
    acc[...] = jnp.zeros_like(acc)
    KB = 1024
    for c in range(CHUNKS):
        for n in range(nt):
            w_copy(c, n).wait()

        def mm(i, _, c=c):
            k = pl.ds(pl.multiple_of(c * 2 * cd + i * KB, KB), KB)
            rhs = jnp.concatenate([wf[n, k, :] for n in range(nt)], axis=1)
            acc[...] += jnp.dot(lk[:, k], rhs, preferred_element_type=F32)
            return 0
        lax.fori_loop(0, 2 * cd // KB, mm, 0)

    keys, values = [], []
    for h in range(nt):
        cs = slice(h * HEAD, (h + 1) * HEAD)
        k = acc[0:M, cs]
        k = (k * cosine + pltpu.roll(k, HEAD // 2, 1) * sine).astype(BF)
        v = acc[M:2 * M, cs].astype(BF)
        kvout[:, cs] = k
        kvout[:, N + h * HEAD:N + (h + 1) * HEAD] = v
        keys.append(k)
        values.append(v)

    def tail(t, _):
        i, j = iota((R * G, M), 0), iota((R * G, M), 1)
        seen = (i // G == lax.rem(j, R)) & (j // R <= t)
        for h in range(nt):
            hs = slice(h * G, (h + 1) * G)
            q = qs[t, :, hs, :].reshape(R * G, HEAD).astype(BF)
            s = lax.dot_general(q, keys[h], (((1,), (1,)), ((), ())), preferred_element_type=F32) * scale
            s = jnp.where(seen, s, -1e30)
            mo = ms[t, :, hs, :].reshape(R * G, HEAD)
            m = jnp.maximum(mo, jnp.max(s, axis=1, keepdims=True))
            p = jnp.exp(s - m[:, :M])
            a = jnp.exp(mo - m)
            l = ls[t, :, hs, :].reshape(R * G, HEAD) * a + jnp.sum(p, axis=1, keepdims=True)
            o = os[t, :, hs, :].reshape(R * G, HEAD) * a + jnp.dot(p.astype(BF), values[h], preferred_element_type=F32)
            os[t, :, hs, :] = (o / l).reshape(R, G, HEAD)
        return 0

    lax.fori_loop(0, T, tail, 0)
    for t in range(T):
        live = (ec[t * R:(t + 1) * R] > sec).astype(F32)
        for j in range(HG):
            out[t, :, j * HEAD:(j + 1) * HEAD] = (os[t, :, j, :] * live).astype(BF)

    for d in range(1, S):
        @pl.when(sec + d < S)
        def _():
            sec_copy(d, sec, lax.rem(sec + d, S)).wait_send()

        @pl.when(sec - d >= 0)
        def _():
            for e in range(1, TP):
                fwd_copy(lax.rem(sec - d + S, S), d, e).wait_send()
    for d in range(1, TP):
        x_copy(d).wait_send()
        g_copy(d).wait_send()


def local(S, TP, hidden, norm_gain, w_kv, queries, cache_kv, exits, lengths):
    T, _, R, Dl = hidden.shape
    _, D, _, N = w_kv.shape
    C = cache_kv.shape[3]
    nt = N // HEAD
    HG = queries.shape[-1] // HEAD
    M = T * R
    slot = 2 * T * EXIT_CAP
    positions = lengths[None, :] + jnp.arange(T, dtype=jnp.int32)[:, None]
    vmem = pl.BlockSpec(memory_space=pltpu.VMEM)
    hbm = pl.BlockSpec(memory_space=pl.ANY)
    dma = pltpu.SemaphoreType.DMA
    attended, fresh = pl.pallas_call(
        functools.partial(kernel, S, TP),
        out_shape=(jax.ShapeDtypeStruct((T, R, HG * HEAD), BF), jax.ShapeDtypeStruct((M, 2 * N), BF)),
        in_specs=[vmem, vmem, hbm, hbm, hbm, vmem, vmem, vmem, pl.BlockSpec(memory_space=pltpu.SMEM)],
        out_specs=(vmem, vmem),
        scratch_shapes=[
            pltpu.VMEM((nt, D, 2, HEAD), BF),
            pltpu.VMEM((R, 2, C, N), BF),
            pltpu.VMEM((T, R, HG * HEAD), BF),
            pltpu.VMEM((T, R, HG, HEAD), F32),
            pltpu.VMEM((T, R, HG, HEAD), F32),
            pltpu.VMEM((T, R, HG, HEAD), F32),
            pltpu.VMEM((T, R, HG, HEAD), F32),
            pltpu.VMEM((TP, T, R, Dl), BF),
            pltpu.VMEM((TP, S * slot, Dl // 2), BF),
            pltpu.VMEM((slot, Dl // 2), BF),
            pltpu.VMEM((8, Dl), F32),
            pltpu.VMEM((TP, 8, Dl), F32),
            pltpu.VMEM((2 * M, 2 * D), BF),
            pltpu.VMEM((2 * M, N), F32),
            dma((CHUNKS, nt)), dma((2,)), dma,
            dma((S - 1,)), dma((S - 1,)),
            dma((TP - 1,)), dma((TP - 1,)), dma((TP - 1,)), dma((TP - 1,)),
            dma((S - 1, TP - 1)), dma((S - 1, TP - 1)),
        ],
        compiler_params=pltpu.CompilerParams(
            collective_id=0, has_side_effects=True, vmem_limit_bytes=56 << 20),
    )(hidden[:, 0], norm_gain, w_kv[0], queries[:, 0], cache_kv[0],
      exits.reshape(M, 1), exits.reshape(1, M), positions.reshape(M, 1), lengths)
    return attended[:, None], fresh.reshape(T, 1, R, 2, N)


def solution(mesh):
    placed = (
        P(None, "section", "req", "tp"),
        P("section", "tp"),
        P("section", None, None, "tp"),
        P(None, "section", "req", "tp"),
        P("section", "req", None, None, "tp"),
        P(None, "req"),
        P("req"),
    )
    return jax.shard_map(
        functools.partial(local, mesh.shape["section"], mesh.shape["tp"]),
        mesh=mesh,
        in_specs=placed,
        out_specs=(P(None, "section", "req", "tp"), P(None, "section", "req", None, "tp")),
        check_vma=False,
    )
```

```python
import functools
import math

import jax
import jax.numpy as jnp
from jax import lax
from jax.experimental import pallas as pl
from jax.experimental.pallas import tpu as pltpu
from jax.sharding import PartitionSpec as P

HEAD = 128
EXIT_CAP = 2
EPSILON = 1e-05
ROPE_BASE = 500000.0
CHUNKS = 4
BF = jnp.bfloat16
F32 = jnp.float32
MESH = pl.DeviceIdType.MESH


def iota(shape, axis):
    return lax.broadcasted_iota(jnp.int32, shape, axis)


def kernel(S, TP, hid, gain, w_hbm, q_hbm, c_hbm, exits, lrow, lens,
           out, kvout,
           wv, cv, qv, qs, os, ms, ls, xf, gb, pack, gsend, gfull, lk, acc,
           wsem, csem, qsem, sec_send, sec_recv, x_send, x_recv, g_send, g_recv, f_send, f_recv):
    T, R, Dl = hid.shape
    D, _, N = w_hbm.shape
    nt = N // HEAD
    M = T * R
    half = Dl // 2
    rows = T * EXIT_CAP
    slot = 2 * rows
    C = c_hbm.shape[2]
    HG = qs.shape[2]
    G = HG // nt
    sec = lax.axis_index("section")
    req = lax.axis_index("req")
    tp = lax.axis_index("tp")

    barrier = pltpu.get_barrier_semaphore()
    for d in range(1, S):
        pl.semaphore_signal(barrier, inc=1, device_id=(lax.rem(sec + d, S), req, tp), device_id_type=MESH)
    for d in range(1, TP):
        pl.semaphore_signal(barrier, inc=1, device_id=(sec, req, lax.rem(tp + d, TP)), device_id_type=MESH)

    q_copy = pltpu.make_async_copy(q_hbm, qv, qsem)
    q_copy.start()
    c_copies = [pltpu.make_async_copy(c_hbm.at[pl.ds(i * (R // 2), R // 2)], cv.at[pl.ds(i * (R // 2), R // 2)], csem.at[i])
                for i in range(2)]
    for c in c_copies:
        c.start()
    cd = D // CHUNKS

    def w_copy(c, n):
        return pltpu.make_async_copy(
            w_hbm.at[pl.ds(c * cd, cd), :, pl.ds(n * HEAD, HEAD)],
            wv.at[n, pl.ds(c * cd, cd)], wsem.at[c, n])

    for c in range(CHUNKS):
        for n in range(nt):
            w_copy(c, n).start()

    ri, rj = iota((M, M), 0), iota((M, M), 1)
    own = iota((M, R), 1) == lax.rem(iota((M, R), 0), R)

    def column(spread):
        return jnp.sum(jnp.where(own, spread.astype(F32), 0.0), axis=1, keepdims=True)

    ecf = column(jnp.concatenate([jnp.broadcast_to(exits[t:t + 1, :], (R, R)) for t in range(T)], axis=0))
    ec = ecf.astype(jnp.int32)
    er = jnp.sum(jnp.where(ri == rj, ecf, 0.0), axis=0, keepdims=True).astype(jnp.int32)
    pos = column(jnp.broadcast_to(lrow[...], (M, R))) + (iota((M, 1), 0) // R).astype(F32)
    same = (ec == er) & (ri // R == rj // R)
    rank_row = jnp.sum((same & (ri < rj)).astype(F32), axis=0, keepdims=True).astype(jnp.int32)
    rank_col = jnp.sum((same & (rj < ri)).astype(F32), axis=1, keepdims=True).astype(jnp.int32)
    pk, pj = iota((rows, M), 0), iota((rows, M), 1)
    pick = ((er == sec) & (pk == (pj // R) * EXIT_CAP + rank_row)).astype(F32).astype(BF)
    hv = hid[...].reshape(M, Dl)
    packed = jnp.dot(pick, hv, preferred_element_type=F32)
    pack[...] = jnp.concatenate([packed[:, :half], packed[:, half:]], axis=0).astype(BF)
    gsend[...] = jnp.broadcast_to(gain[...].astype(F32), gsend.shape)
    pl.semaphore_wait(barrier, S - 1 + TP - 1)

    def sec_copy(d, src, target):
        return pltpu.make_async_remote_copy(
            src_ref=pack, dst_ref=gb.at[tp, pl.ds(src * slot, slot)],
            send_sem=sec_send.at[d - 1], recv_sem=sec_recv.at[d - 1],
            device_id=(target, req, tp), device_id_type=MESH)

    for d in range(1, S):
        @pl.when(sec + d < S)
        def _():
            sec_copy(d, sec, lax.rem(sec + d, S)).start()

    def x_copy(d):
        return pltpu.make_async_remote_copy(
            src_ref=hid, dst_ref=xf.at[tp], send_sem=x_send.at[d - 1], recv_sem=x_recv.at[d - 1],
            device_id=(sec, req, lax.rem(tp + d, TP)), device_id_type=MESH)

    def g_copy(d):
        return pltpu.make_async_remote_copy(
            src_ref=gsend, dst_ref=gfull.at[tp], send_sem=g_send.at[d - 1], recv_sem=g_recv.at[d - 1],
            device_id=(sec, req, lax.rem(tp + d, TP)), device_id_type=MESH)

    for d in range(1, TP):
        x_copy(d).start()
        g_copy(d).start()
    xf[tp] = hid[...]
    gfull[tp] = gsend[...]
    for s in range(S):
        @pl.when(s >= sec)
        def _():
            gb[:, s * slot:(s + 1) * slot, :] = jnp.zeros((TP, slot, half), BF)

    def fwd_copy(s, o, d):
        span = pl.ds(s * slot, slot)
        return pltpu.make_async_remote_copy(
            src_ref=gb.at[tp, span], dst_ref=gb.at[tp, span],
            send_sem=f_send.at[o - 1, d - 1], recv_sem=f_recv.at[o - 1, d - 1],
            device_id=(sec, req, lax.rem(tp + d, TP)), device_id_type=MESH)

    q_copy.wait()
    for t in range(T):
        for j in range(HG):
            qs[t, :, j, :] = qv[t, :, j * HEAD:(j + 1) * HEAD].astype(F32)

    for d in range(1, S):
        @pl.when(sec - d >= 0)
        def _():
            s = lax.rem(sec - d + S, S)
            sec_copy(d, s, lax.rem(sec + d, S)).wait_recv()
            for e in range(1, TP):
                fwd_copy(s, d, e).start()

    for c in c_copies:
        c.wait()
    scale = HEAD ** -0.5
    RB = 4
    TG = T * G

    def old(i, _):
        pairs = [(b, h) for b in range(RB) for h in range(nt)]
        scores = []
        for b, h in pairs:
            r = i * RB + b
            qh = jnp.concatenate([qs[t, r, h * G:(h + 1) * G, :] for t in range(T)], axis=0).astype(BF)
            s = lax.dot_general(qh, cv[r, 0, :, h * HEAD:(h + 1) * HEAD], (((1,), (1,)), ((), ())), preferred_element_type=F32) * scale
            scores.append(jnp.where(iota((TG, C), 1) < lens[r], s, -1e30))
        s = jnp.concatenate(scores, axis=0)
        m = jnp.max(s, axis=1, keepdims=True)
        p = jnp.exp(s - m)
        l = jnp.broadcast_to(jnp.sum(p, axis=1, keepdims=True), (len(pairs) * TG, HEAD))
        m = jnp.broadcast_to(m, (len(pairs) * TG, HEAD))
        p = p.astype(BF)
        for k, (b, h) in enumerate(pairs):
            r = i * RB + b
            o = jnp.dot(p[k * TG:(k + 1) * TG], cv[r, 1, :, h * HEAD:(h + 1) * HEAD], preferred_element_type=F32)
            for t in range(T):
                hs = slice(h * G, (h + 1) * G)
                g = slice(k * TG + t * G, k * TG + (t + 1) * G)
                os[t, r, hs, :] = o[t * G:(t + 1) * G]
                ms[t, r, hs, :] = m[g]
                ls[t, r, hs, :] = l[g]
        return 0

    lax.fori_loop(0, R // RB, old, 0)

    lane = iota((M, HEAD), 1)
    exponent = lax.rem(lane, HEAD // 2).astype(F32) * (2.0 / HEAD)
    angle = pos * jnp.exp(exponent * (-math.log(ROPE_BASE)))
    cosine = jnp.cos(angle)
    sine = jnp.where(lane < HEAD // 2, -1.0, 1.0) * jnp.sin(angle)

    for d in range(1, TP):
        x_copy(d).wait_recv()
        g_copy(d).wait_recv()
    for d in range(1, S):
        @pl.when(sec - d >= 0)
        def _():
            for e in range(1, TP):
                fwd_copy(lax.rem(sec - d + S, S), d, e).wait_recv()

    want = ec * slot + (iota((M, 1), 0) // R) * EXIT_CAP + rank_col
    skipped = ec < sec
    W = min(half, 2048)
    total = jnp.zeros((M, HEAD), F32)
    for f in range(2):
        choose = (iota((M, S * slot), 1) == want + f * rows).astype(F32).astype(BF)
        for p in range(TP):
            def part(i, total, f=f, p=p, choose=choose):
                gc = pl.ds(pl.multiple_of(i * W, W), W)
                xc = pl.ds(pl.multiple_of(f * half + i * W, W), W)
                came = jnp.dot(choose, gb[p, :, gc], preferred_element_type=F32)
                src = jnp.where(skipped, came, xf[p, :, :, xc].reshape(M, W).astype(F32))
                xf[p, :, :, xc] = src.astype(BF).reshape(T, R, W)
                for k in range(W // HEAD):
                    v = src[:, k * HEAD:(k + 1) * HEAD]
                    total = total + v * v
                return total
            total = lax.fori_loop(0, half // W, part, total)
    inverse = lax.rsqrt(jnp.sum(total, axis=1, keepdims=True) / D + EPSILON)

    er_, ec_ = iota((HEAD, 2 * HEAD), 0), iota((HEAD, 2 * HEAD), 1)
    even = (ec_ == 2 * er_).astype(F32).astype(BF)
    odd = (ec_ == 2 * er_ + 1).astype(F32).astype(BF)
    B = min(16, Dl // HEAD)
    for p in range(TP):
        def expand(i, _, p=p):
            parts = []
            for b in range(B):
                cols = pl.ds(pl.multiple_of((i * B + b) * HEAD, HEAD), HEAD)
                v = xf[p, :, :, cols].reshape(M, HEAD).astype(F32) * inverse * gfull[p, 0:1, cols]
                parts.append(v.astype(BF))
            x = jnp.concatenate(parts, axis=0)
            a = jnp.dot(x, even, preferred_element_type=F32).astype(BF)
            c = jnp.dot(x, odd, preferred_element_type=F32).astype(BF)
            for b in range(B):
                cols = pl.ds(pl.multiple_of((p * (Dl // HEAD) + i * B + b) * 2 * HEAD, 2 * HEAD), 2 * HEAD)
                lk[0:M, cols] = a[b * M:(b + 1) * M]
                lk[M:2 * M, cols] = c[b * M:(b + 1) * M]
            return 0
        lax.fori_loop(0, Dl // HEAD // B, expand, 0)

    wf = wv.reshape(nt, 2 * D, HEAD)
    acc[...] = jnp.zeros_like(acc)
    KB = 2048
    for c in range(CHUNKS):
        for n in range(nt):
            w_copy(c, n).wait()

        def mm(i, _, c=c):
            k = pl.ds(pl.multiple_of(c * 2 * cd + i * KB, KB), KB)
            rhs = jnp.concatenate([wf[n, k, :] for n in range(nt)], axis=1)
            acc[...] += jnp.dot(lk[:, k], rhs, preferred_element_type=F32)
            return 0
        lax.fori_loop(0, 2 * cd // KB, mm, 0)

    keys, values = [], []
    for h in range(nt):
        cs = slice(h * HEAD, (h + 1) * HEAD)
        k = acc[0:M, cs]
        k = (k * cosine + pltpu.roll(k, HEAD // 2, 1) * sine).astype(BF)
        v = acc[M:2 * M, cs].astype(BF)
        kvout[:, cs] = k
        kvout[:, N + h * HEAD:N + (h + 1) * HEAD] = v
        keys.append(k)
        values.append(v)

    def tail(t, _):
        i, j = iota((R * G, M), 0), iota((R * G, M), 1)
        seen = (i // G == lax.rem(j, R)) & (j // R <= t)
        for h in range(nt):
            hs = slice(h * G, (h + 1) * G)
            q = qs[t, :, hs, :].reshape(R * G, HEAD).astype(BF)
            s = lax.dot_general(q, keys[h], (((1,), (1,)), ((), ())), preferred_element_type=F32) * scale
            s = jnp.where(seen, s, -1e30)
            mo = ms[t, :, hs, :].reshape(R * G, HEAD)
            m = jnp.maximum(mo, jnp.max(s, axis=1, keepdims=True))
            p = jnp.exp(s - m[:, :M])
            a = jnp.exp(mo - m)
            l = ls[t, :, hs, :].reshape(R * G, HEAD) * a + jnp.sum(p, axis=1, keepdims=True)
            o = os[t, :, hs, :].reshape(R * G, HEAD) * a + jnp.dot(p.astype(BF), values[h], preferred_element_type=F32)
            os[t, :, hs, :] = (o / l).reshape(R, G, HEAD)
        return 0

    lax.fori_loop(0, T, tail, 0)
    for t in range(T):
        live = (ec[t * R:(t + 1) * R] > sec).astype(F32)
        for j in range(HG):
            out[t, :, j * HEAD:(j + 1) * HEAD] = (os[t, :, j, :] * live).astype(BF)

    for d in range(1, S):
        @pl.when(sec + d < S)
        def _():
            sec_copy(d, sec, lax.rem(sec + d, S)).wait_send()

        @pl.when(sec - d >= 0)
        def _():
            for e in range(1, TP):
                fwd_copy(lax.rem(sec - d + S, S), d, e).wait_send()
    for d in range(1, TP):
        x_copy(d).wait_send()
        g_copy(d).wait_send()


def local(S, TP, hidden, norm_gain, w_kv, queries, cache_kv, exits, lengths):
    T, _, R, Dl = hidden.shape
    _, D, _, N = w_kv.shape
    C = cache_kv.shape[3]
    nt = N // HEAD
    HG = queries.shape[-1] // HEAD
    M = T * R
    slot = 2 * T * EXIT_CAP
    vmem = pl.BlockSpec(memory_space=pltpu.VMEM)
    hbm = pl.BlockSpec(memory_space=pl.ANY)
    dma = pltpu.SemaphoreType.DMA
    attended, fresh = pl.pallas_call(
        functools.partial(kernel, S, TP),
        out_shape=(jax.ShapeDtypeStruct((T, R, HG * HEAD), BF), jax.ShapeDtypeStruct((M, 2 * N), BF)),
        in_specs=[vmem, vmem, hbm, hbm, hbm, vmem, vmem, pl.BlockSpec(memory_space=pltpu.SMEM)],
        out_specs=(vmem, vmem),
        scratch_shapes=[
            pltpu.VMEM((nt, D, 2, HEAD), BF),
            pltpu.VMEM((R, 2, C, N), BF),
            pltpu.VMEM((T, R, HG * HEAD), BF),
            pltpu.VMEM((T, R, HG, HEAD), F32),
            pltpu.VMEM((T, R, HG, HEAD), F32),
            pltpu.VMEM((T, R, HG, HEAD), F32),
            pltpu.VMEM((T, R, HG, HEAD), F32),
            pltpu.VMEM((TP, T, R, Dl), BF),
            pltpu.VMEM((TP, S * slot, Dl // 2), BF),
            pltpu.VMEM((slot, Dl // 2), BF),
            pltpu.VMEM((8, Dl), F32),
            pltpu.VMEM((TP, 8, Dl), F32),
            pltpu.VMEM((2 * M, 2 * D), BF),
            pltpu.VMEM((2 * M, N), F32),
            dma((CHUNKS, nt)), dma((2,)), dma,
            dma((S - 1,)), dma((S - 1,)),
            dma((TP - 1,)), dma((TP - 1,)), dma((TP - 1,)), dma((TP - 1,)),
            dma((S - 1, TP - 1)), dma((S - 1, TP - 1)),
        ],
        compiler_params=pltpu.CompilerParams(
            collective_id=0, has_side_effects=True, vmem_limit_bytes=56 << 20),
    )(hidden[:, 0], norm_gain, w_kv[0], queries[:, 0], cache_kv[0],
      exits, lengths.reshape(1, R), lengths)
    return attended[:, None], fresh.reshape(T, 1, R, 2, N)


def solution(mesh):
    placed = (
        P(None, "section", "req", "tp"),
        P("section", "tp"),
        P("section", None, None, "tp"),
        P(None, "section", "req", "tp"),
        P("section", "req", None, None, "tp"),
        P(None, "req"),
        P("req"),
    )
    return jax.shard_map(
        functools.partial(local, mesh.shape["section"], mesh.shape["tp"]),
        mesh=mesh,
        in_specs=placed,
        out_specs=(P(None, "section", "req", "tp"), P(None, "section", "req", None, "tp")),
        check_vma=False,
    )
```

```python
import functools
import math

import jax
import jax.numpy as jnp
from jax import lax
from jax.experimental import pallas as pl
from jax.experimental.pallas import tpu as pltpu
from jax.sharding import PartitionSpec as P

HEAD = 128
EXIT_CAP = 2
EPSILON = 1e-05
ROPE_BASE = 500000.0
CHUNKS = 4
BF = jnp.bfloat16
F32 = jnp.float32
MESH = pl.DeviceIdType.MESH


def iota(shape, axis):
    return lax.broadcasted_iota(jnp.int32, shape, axis)


def kernel(S, TP, hid, gain, w_hbm, q_hbm, c_hbm, exits, lrow, lens,
           out, kvout,
           wv, cv, qv, qs, os, ms, ls, xf, gb, pack, gsend, gfull, lk, acc,
           wsem, csem, qsem, sec_send, sec_recv, x_send, x_recv, g_send, g_recv, f_send, f_recv):
    T, R, Dl = hid.shape
    D, _, N = w_hbm.shape
    nt = N // HEAD
    M = T * R
    half = Dl // 2
    rows = T * EXIT_CAP
    slot = 2 * rows
    C = c_hbm.shape[2]
    HG = qs.shape[2]
    G = HG // nt
    sec = lax.axis_index("section")
    req = lax.axis_index("req")
    tp = lax.axis_index("tp")

    barrier = pltpu.get_barrier_semaphore()
    for d in range(1, S):
        pl.semaphore_signal(barrier, inc=1, device_id=(lax.rem(sec + d, S), req, tp), device_id_type=MESH)
    for d in range(1, TP):
        pl.semaphore_signal(barrier, inc=1, device_id=(sec, req, lax.rem(tp + d, TP)), device_id_type=MESH)

    q_copy = pltpu.make_async_copy(q_hbm, qv, qsem)
    q_copy.start()
    c_copies = [pltpu.make_async_copy(c_hbm.at[pl.ds(i * (R // 2), R // 2)], cv.at[pl.ds(i * (R // 2), R // 2)], csem.at[i])
                for i in range(2)]
    for c in c_copies:
        c.start()
    cd = D // CHUNKS

    def w_copy(c, n):
        return pltpu.make_async_copy(
            w_hbm.at[pl.ds(c * cd, cd), :, pl.ds(n * HEAD, HEAD)],
            wv.at[n, pl.ds(c * cd, cd)], wsem.at[c, n])

    for c in range(CHUNKS):
        for n in range(nt):
            w_copy(c, n).start()

    ri, rj = iota((M, M), 0), iota((M, M), 1)
    own = iota((M, R), 1) == lax.rem(iota((M, R), 0), R)

    def column(spread):
        return jnp.sum(jnp.where(own, spread.astype(F32), 0.0), axis=1, keepdims=True)

    ecf = column(jnp.concatenate([jnp.broadcast_to(exits[t:t + 1, :], (R, R)) for t in range(T)], axis=0))
    ec = ecf.astype(jnp.int32)
    er = jnp.sum(jnp.where(ri == rj, ecf, 0.0), axis=0, keepdims=True).astype(jnp.int32)
    pos = column(jnp.broadcast_to(lrow[...], (M, R))) + (iota((M, 1), 0) // R).astype(F32)
    same = (ec == er) & (ri // R == rj // R)
    rank_row = jnp.sum((same & (ri < rj)).astype(F32), axis=0, keepdims=True).astype(jnp.int32)
    rank_col = jnp.sum((same & (rj < ri)).astype(F32), axis=1, keepdims=True).astype(jnp.int32)
    pk, pj = iota((rows, M), 0), iota((rows, M), 1)
    pick = ((er == sec) & (pk == (pj // R) * EXIT_CAP + rank_row)).astype(F32).astype(BF)
    hv = hid[...].reshape(M, Dl)
    packed = jnp.dot(pick, hv, preferred_element_type=F32)
    pack[...] = jnp.concatenate([packed[:, :half], packed[:, half:]], axis=0).astype(BF)
    gsend[...] = jnp.broadcast_to(gain[...].astype(F32), gsend.shape)
    pl.semaphore_wait(barrier, S - 1 + TP - 1)

    def sec_copy(d, src, target):
        return pltpu.make_async_remote_copy(
            src_ref=pack, dst_ref=gb.at[tp, pl.ds(src * slot, slot)],
            send_sem=sec_send.at[d - 1], recv_sem=sec_recv.at[d - 1],
            device_id=(target, req, tp), device_id_type=MESH)

    for d in range(1, S):
        @pl.when(sec + d < S)
        def _():
            sec_copy(d, sec, lax.rem(sec + d, S)).start()

    def x_copy(d):
        return pltpu.make_async_remote_copy(
            src_ref=hid, dst_ref=xf.at[tp], send_sem=x_send.at[d - 1], recv_sem=x_recv.at[d - 1],
            device_id=(sec, req, lax.rem(tp + d, TP)), device_id_type=MESH)

    def g_copy(d):
        return pltpu.make_async_remote_copy(
            src_ref=gsend, dst_ref=gfull.at[tp], send_sem=g_send.at[d - 1], recv_sem=g_recv.at[d - 1],
            device_id=(sec, req, lax.rem(tp + d, TP)), device_id_type=MESH)

    for d in range(1, TP):
        x_copy(d).start()
        g_copy(d).start()
    xf[tp] = hid[...]
    gfull[tp] = gsend[...]
    for s in range(S):
        @pl.when(s >= sec)
        def _():
            gb[:, s * slot:(s + 1) * slot, :] = jnp.zeros((TP, slot, half), BF)

    def fwd_copy(s, o, d):
        span = pl.ds(s * slot, slot)
        return pltpu.make_async_remote_copy(
            src_ref=gb.at[tp, span], dst_ref=gb.at[tp, span],
            send_sem=f_send.at[o - 1, d - 1], recv_sem=f_recv.at[o - 1, d - 1],
            device_id=(sec, req, lax.rem(tp + d, TP)), device_id_type=MESH)

    q_copy.wait()
    for t in range(T):
        for j in range(HG):
            qs[t, :, j, :] = qv[t, :, j * HEAD:(j + 1) * HEAD].astype(F32)

    for d in range(1, S):
        @pl.when(sec - d >= 0)
        def _():
            s = lax.rem(sec - d + S, S)
            sec_copy(d, s, lax.rem(sec + d, S)).wait_recv()
            for e in range(1, TP):
                fwd_copy(s, d, e).start()

    for c in c_copies:
        c.wait()
    scale = HEAD ** -0.5
    RB = 4
    TG = T * G

    def old(i, _):
        pairs = [(b, h) for b in range(RB) for h in range(nt)]
        scores = []
        for b, h in pairs:
            r = i * RB + b
            qh = jnp.concatenate([qs[t, r, h * G:(h + 1) * G, :] for t in range(T)], axis=0).astype(BF)
            s = lax.dot_general(qh, cv[r, 0, :, h * HEAD:(h + 1) * HEAD], (((1,), (1,)), ((), ())), preferred_element_type=F32) * scale
            scores.append(jnp.where(iota((TG, C), 1) < lens[r], s, -1e30))
        s = jnp.concatenate(scores, axis=0)
        m = jnp.max(s, axis=1, keepdims=True)
        p = jnp.exp(s - m)
        l = jnp.broadcast_to(jnp.sum(p, axis=1, keepdims=True), (len(pairs) * TG, HEAD))
        m = jnp.broadcast_to(m, (len(pairs) * TG, HEAD))
        p = p.astype(BF)
        for k, (b, h) in enumerate(pairs):
            r = i * RB + b
            o = jnp.dot(p[k * TG:(k + 1) * TG], cv[r, 1, :, h * HEAD:(h + 1) * HEAD], preferred_element_type=F32)
            for t in range(T):
                hs = slice(h * G, (h + 1) * G)
                g = slice(k * TG + t * G, k * TG + (t + 1) * G)
                os[t, r, hs, :] = o[t * G:(t + 1) * G]
                ms[t, r, hs, :] = m[g]
                ls[t, r, hs, :] = l[g]
        return 0

    lax.fori_loop(0, R // RB, old, 0)

    lane = iota((M, HEAD), 1)
    exponent = lax.rem(lane, HEAD // 2).astype(F32) * (2.0 / HEAD)
    angle = pos * jnp.exp(exponent * (-math.log(ROPE_BASE)))
    cosine = jnp.cos(angle)
    sine = jnp.where(lane < HEAD // 2, -1.0, 1.0) * jnp.sin(angle)

    for d in range(1, TP):
        x_copy(d).wait_recv()
        g_copy(d).wait_recv()
    for d in range(1, S):
        @pl.when(sec - d >= 0)
        def _():
            for e in range(1, TP):
                fwd_copy(lax.rem(sec - d + S, S), d, e).wait_recv()

    want = ec * slot + (iota((M, 1), 0) // R) * EXIT_CAP + rank_col
    skipped = ec < sec
    W = min(half, 2048)
    total = jnp.zeros((M, HEAD), F32)
    for f in range(2):
        choose = (iota((M, S * slot), 1) == want + f * rows).astype(F32).astype(BF)
        for p in range(TP):
            def part(i, total, f=f, p=p, choose=choose):
                gc = pl.ds(pl.multiple_of(i * W, W), W)
                xc = pl.ds(pl.multiple_of(f * half + i * W, W), W)
                came = jnp.dot(choose, gb[p, :, gc], preferred_element_type=F32)
                src = jnp.where(skipped, came, xf[p, :, :, xc].reshape(M, W).astype(F32))
                xf[p, :, :, xc] = src.astype(BF).reshape(T, R, W)
                for k in range(W // HEAD):
                    v = src[:, k * HEAD:(k + 1) * HEAD]
                    total = total + v * v
                return total
            total = lax.fori_loop(0, half // W, part, total)
    inverse = lax.rsqrt(jnp.sum(total, axis=1, keepdims=True) / D + EPSILON)

    er_, ec_ = iota((HEAD, 2 * HEAD), 0), iota((HEAD, 2 * HEAD), 1)
    even = (ec_ == 2 * er_).astype(F32).astype(BF)
    odd = (ec_ == 2 * er_ + 1).astype(F32).astype(BF)
    B = min(16, Dl // HEAD)
    for p in range(TP):
        def expand(i, _, p=p):
            parts = []
            for b in range(B):
                cols = pl.ds(pl.multiple_of((i * B + b) * HEAD, HEAD), HEAD)
                v = xf[p, :, :, cols].reshape(M, HEAD).astype(F32) * inverse * gfull[p, 0:1, cols]
                parts.append(v.astype(BF))
            x = jnp.concatenate(parts, axis=0)
            a = jnp.dot(x, even, preferred_element_type=F32).astype(BF)
            c = jnp.dot(x, odd, preferred_element_type=F32).astype(BF)
            for b in range(B):
                cols = pl.ds(pl.multiple_of((p * (Dl // HEAD) + i * B + b) * 2 * HEAD, 2 * HEAD), 2 * HEAD)
                lk[0:M, cols] = a[b * M:(b + 1) * M]
                lk[M:2 * M, cols] = c[b * M:(b + 1) * M]
            return 0
        lax.fori_loop(0, Dl // HEAD // B, expand, 0)

    wf = wv.reshape(nt, 2 * D, HEAD)
    acc[...] = jnp.zeros_like(acc)
    KB = 2 * cd
    for c in range(CHUNKS):
        for n in range(nt):
            w_copy(c, n).wait()

        def mm(i, _, c=c):
            k = pl.ds(pl.multiple_of(c * 2 * cd + i * KB, KB), KB)
            rhs = jnp.concatenate([wf[n, k, :] for n in range(nt)], axis=1)
            acc[...] += jnp.dot(lk[:, k], rhs, preferred_element_type=F32)
            return 0
        lax.fori_loop(0, 2 * cd // KB, mm, 0)

    keys, values = [], []
    for h in range(nt):
        cs = slice(h * HEAD, (h + 1) * HEAD)
        k = acc[0:M, cs]
        k = (k * cosine + pltpu.roll(k, HEAD // 2, 1) * sine).astype(BF)
        v = acc[M:2 * M, cs].astype(BF)
        kvout[:, cs] = k
        kvout[:, N + h * HEAD:N + (h + 1) * HEAD] = v
        keys.append(k)
        values.append(v)

    def tail(t, _):
        RG = R * G
        i, j = iota((nt * RG, M), 0), iota((nt * RG, M), 1)
        seen = (lax.rem(i, RG) // G == lax.rem(j, R)) & (j // R <= t)

        def rows_of(ref):
            return [ref[t, :, h * G:(h + 1) * G, :].reshape(RG, HEAD) for h in range(nt)]

        s = jnp.concatenate([
            lax.dot_general(q.astype(BF), keys[h], (((1,), (1,)), ((), ())), preferred_element_type=F32)
            for h, q in enumerate(rows_of(qs))], axis=0) * scale
        s = jnp.where(seen, s, -1e30)
        mo = jnp.concatenate(rows_of(ms), axis=0)
        m = jnp.maximum(mo, jnp.max(s, axis=1, keepdims=True))
        p = jnp.exp(s - m[:, :M])
        a = jnp.exp(mo - m)
        l = jnp.concatenate(rows_of(ls), axis=0) * a + jnp.sum(p, axis=1, keepdims=True)
        p = p.astype(BF)
        new = jnp.concatenate([
            jnp.dot(p[h * RG:(h + 1) * RG], values[h], preferred_element_type=F32) for h in range(nt)], axis=0)
        o = (jnp.concatenate(rows_of(os), axis=0) * a + new) / l
        for h in range(nt):
            os[t, :, h * G:(h + 1) * G, :] = o[h * RG:(h + 1) * RG].reshape(R, G, HEAD)
        return 0

    lax.fori_loop(0, T, tail, 0)
    for t in range(T):
        live = (ec[t * R:(t + 1) * R] > sec).astype(F32)
        for j in range(HG):
            out[t, :, j * HEAD:(j + 1) * HEAD] = (os[t, :, j, :] * live).astype(BF)

    for d in range(1, S):
        @pl.when(sec + d < S)
        def _():
            sec_copy(d, sec, lax.rem(sec + d, S)).wait_send()

        @pl.when(sec - d >= 0)
        def _():
            for e in range(1, TP):
                fwd_copy(lax.rem(sec - d + S, S), d, e).wait_send()
    for d in range(1, TP):
        x_copy(d).wait_send()
        g_copy(d).wait_send()


def local(S, TP, hidden, norm_gain, w_kv, queries, cache_kv, exits, lengths):
    T, _, R, Dl = hidden.shape
    _, D, _, N = w_kv.shape
    C = cache_kv.shape[3]
    nt = N // HEAD
    HG = queries.shape[-1] // HEAD
    M = T * R
    slot = 2 * T * EXIT_CAP
    vmem = pl.BlockSpec(memory_space=pltpu.VMEM)
    hbm = pl.BlockSpec(memory_space=pl.ANY)
    dma = pltpu.SemaphoreType.DMA
    attended, fresh = pl.pallas_call(
        functools.partial(kernel, S, TP),
        out_shape=(jax.ShapeDtypeStruct((T, R, HG * HEAD), BF), jax.ShapeDtypeStruct((M, 2 * N), BF)),
        in_specs=[vmem, vmem, hbm, hbm, hbm, vmem, vmem, pl.BlockSpec(memory_space=pltpu.SMEM)],
        out_specs=(vmem, vmem),
        scratch_shapes=[
            pltpu.VMEM((nt, D, 2, HEAD), BF),
            pltpu.VMEM((R, 2, C, N), BF),
            pltpu.VMEM((T, R, HG * HEAD), BF),
            pltpu.VMEM((T, R, HG, HEAD), F32),
            pltpu.VMEM((T, R, HG, HEAD), F32),
            pltpu.VMEM((T, R, HG, HEAD), F32),
            pltpu.VMEM((T, R, HG, HEAD), F32),
            pltpu.VMEM((TP, T, R, Dl), BF),
            pltpu.VMEM((TP, S * slot, Dl // 2), BF),
            pltpu.VMEM((slot, Dl // 2), BF),
            pltpu.VMEM((8, Dl), F32),
            pltpu.VMEM((TP, 8, Dl), F32),
            pltpu.VMEM((2 * M, 2 * D), BF),
            pltpu.VMEM((2 * M, N), F32),
            dma((CHUNKS, nt)), dma((2,)), dma,
            dma((S - 1,)), dma((S - 1,)),
            dma((TP - 1,)), dma((TP - 1,)), dma((TP - 1,)), dma((TP - 1,)),
            dma((S - 1, TP - 1)), dma((S - 1, TP - 1)),
        ],
        compiler_params=pltpu.CompilerParams(
            collective_id=0, has_side_effects=True, vmem_limit_bytes=56 << 20),
    )(hidden[:, 0], norm_gain, w_kv[0], queries[:, 0], cache_kv[0],
      exits, lengths.reshape(1, R), lengths)
    return attended[:, None], fresh.reshape(T, 1, R, 2, N)


def solution(mesh):
    placed = (
        P(None, "section", "req", "tp"),
        P("section", "tp"),
        P("section", None, None, "tp"),
        P(None, "section", "req", "tp"),
        P("section", "req", None, None, "tp"),
        P(None, "req"),
        P("req"),
    )
    return jax.shard_map(
        functools.partial(local, mesh.shape["section"], mesh.shape["tp"]),
        mesh=mesh,
        in_specs=placed,
        out_specs=(P(None, "section", "req", "tp"), P(None, "section", "req", None, "tp")),
        check_vma=False,
    )
```
